768 devices in a mesh: dp: 24 (over x, z_lo), expert: 32 (over z_hi, y, core).
Axes of the slice: x: 4, y: 8, z: 12 (z_hi: 2, z_lo: 6; z = z_hi * 6 + z_lo), core: 2. Of those that a mesh axis runs over, the one named last changes fastest.
Arguments:
- tokens: bfloat16 [6144, 3072], P(('dp', 'expert')), may hold values from -24 to 24
- row_gate: bfloat16 [6144], P(('dp', 'expert')), may hold values from 0.19921875 to 1
- block_mask: int32 [48], P('dp'), may hold values 0 or 1
- weights: bfloat16 [3, 5376, 3072], P(None, 'expert'), may hold values from -0.109375 to 0.109375
- out_grad: bfloat16 [6144, 3072], P(('dp', 'expert')), may hold values from -24 to 24
Outputs:
- mixed: bfloat16 [6144, 3072], P(('dp', 'expert'))
- token_grad: bfloat16 [6144, 3072], P(('dp', 'expert'))
- weight_grad: bfloat16 [3, 5376, 3072], P(None, 'expert', 'dp')
The draws below stay inside these ranges and needn't reach their ends.
All inputs are finite; a program needn't handle non-finite values. No bound on the sum of `block_mask` on one device may be relied on, other than what follows from the above.
Results may differ from the reference program's by a relative error of at most 0.025.
Values may be sent and summed in bfloat16 or wider, within the bound.
A program may use at most 64 MiB of HBM per device.

```python
import jax
import jax.numpy as jnp
from jax import lax

D = 3072
FF = 5376
GROUP = 256
BLOCK = 128
TOKENS = 6144
BLOCKS = 48
N_DP = 24
N_EXPERT = 32


def set_ends(values, own_key, low, high):
    longest = values.shape.index(max(values.shape))
    spots = []
    for shift in (0, 1):
        where = [jax.random.randint(jax.random.fold_in(own_key, axis), (), 0, length) for axis, length in enumerate(values.shape)]
        where[longest] = (where[longest] + shift) % values.shape[longest]
        spots.append(tuple(where))
    return values.at[spots[0]].set(low).at[spots[1]].set(high)


def strengthened(values, key, source, target, parts, factor):
    owner, partner = [(jnp.arange(values.shape[position]) // (values.shape[position] // parts)).reshape([-1 if axis == position else 1 for axis in range(values.ndim)]) for position in (source, target)]
    chosen = jax.random.permutation(key, parts)[partner]
    strong = (owner == chosen) | (owner == (partner + parts // 2) % parts)
    return jnp.where(strong, factor * values, values)


def block_levels(stream_key, dims, split, smallest, high):
    def one(dim, shards_of):
        steps = jax.random.uniform(jax.random.fold_in(jax.random.fold_in(stream_key, 6), dim), (shards_of,), jnp.float32, smallest / len(split), high / len(split))
        return jnp.repeat(jnp.exp(steps), dims[dim] // shards_of).reshape((-1,) + (1,) * (len(dims) - dim - 1))

    level = one(*split[0])
    for cut in split[1:]:
        level = level * one(*cut)
    return level


def scatter_about(stream_key, shape, deviation, limit, split=(), held_as=jnp.bfloat16):
    array = jax.random.normal(stream_key, shape, jnp.float32) * deviation
    if len(split) > 0:
        array = block_levels(stream_key, shape, split, -0.22, 0.18) * array
    return jnp.clip(array, min=-limit, max=limit).astype(held_as)


def heavy_noise(key, extent, deviation, most, shards, heavy, kind=jnp.bfloat16):
    values = deviation * jax.random.normal(key, extent, jnp.float32)
    if shards:
        values = values * block_levels(key, extent, shards, -0.22, 0.18)
    return jnp.clip(strengthened(values, jax.random.fold_in(key, 3), *heavy), -most, most).astype(kind)


def setup_inputs(seed: int = 0) -> dict:
    seeds = jax.random.split(jax.random.key(seed), 6)
    return {
        "tokens": heavy_noise(seeds[0], (TOKENS, D), 1.0, 24.0, ((0, 768),), (0, 1, 768, 6.0)),
        "row_gate": jnp.clip(0.19921875 + 0.80078125 * jax.random.uniform(seeds[1], (TOKENS,), jnp.float32) ** block_levels(seeds[1], (TOKENS,), ((0, 768),), -0.2, 0.2), 0.19921875, 1.0).astype(jnp.bfloat16),
        "block_mask": set_ends((jax.random.randint(seeds[2], (BLOCKS,), 0, 3) < 2).astype(jnp.int32), jax.random.fold_in(seeds[2], 1), 0, 1),
        "weights": scatter_about(seeds[3], (3, FF, D), D ** -0.5, 0.109375, ((1, 32),)),
        "out_grad": heavy_noise(seeds[4], (TOKENS, D), 1.0, 24.0, ((0, 768),), (0, 1, 768, 6.0)),
    }


def rounded(value):
    return lax.optimization_barrier(value.astype(jnp.bfloat16)).astype(jnp.float32)


def reference(tokens, row_gate, block_mask, weights, out_grad):
    combine = row_gate.astype(jnp.float32)
    row_live = jnp.repeat(block_mask.astype(jnp.float32), BLOCK)[:, None]
    rows_grad = (combine[:, None] * out_grad.astype(jnp.float32)).astype(jnp.bfloat16)
    pre_gate = jnp.dot(tokens, weights[0].T, preferred_element_type=jnp.float32)
    pre_up = jnp.dot(tokens, weights[1].T, preferred_element_type=jnp.float32)
    sigmoid_gate = jax.nn.sigmoid(pre_gate)
    silu_gate = pre_gate * sigmoid_gate
    hidden = (row_live * silu_gate * pre_up).astype(jnp.bfloat16)
    back_hidden = jnp.dot(rows_grad, weights[2].T, preferred_element_type=jnp.float32)
    slope = sigmoid_gate * (1.0 + pre_gate * (1.0 - sigmoid_gate))
    gate_grad = (row_live * back_hidden * pre_up * slope).astype(jnp.bfloat16)
    up_grad = (row_live * back_hidden * silu_gate).astype(jnp.bfloat16)
    local_width = FF // N_EXPERT

    def slice_sums(carry, index):
        start = (index * local_width).astype(jnp.int32)
        hidden_part = lax.dynamic_slice_in_dim(hidden, start, local_width, 1)
        gate_part = lax.dynamic_slice_in_dim(gate_grad, start, local_width, 1)
        up_part = lax.dynamic_slice_in_dim(up_grad, start, local_width, 1)
        w_gate = lax.dynamic_slice_in_dim(weights[0], start, local_width, 0)
        w_up = lax.dynamic_slice_in_dim(weights[1], start, local_width, 0)
        w_down = lax.dynamic_slice_in_dim(weights[2], start, local_width, 0)
        out_term = jnp.dot(hidden_part, w_down, preferred_element_type=jnp.float32)
        in_term = jnp.dot(gate_part, w_gate, preferred_element_type=jnp.float32) + jnp.dot(up_part, w_up, preferred_element_type=jnp.float32)
        return (carry[0] + rounded(out_term), carry[1] + rounded(in_term)), None

    zeros = jnp.zeros((TOKENS, D), jnp.float32)
    sums, unused = lax.scan(slice_sums, (zeros, zeros), jnp.arange(N_EXPERT, dtype=jnp.int32))
    out_sum, in_sum = sums
    mixed = (combine[:, None] * out_sum).astype(jnp.bfloat16)
    token_grad = in_sum.astype(jnp.bfloat16)

    def group_sums(carry, index):
        start = (index * GROUP).astype(jnp.int32)
        rows = lax.dynamic_slice_in_dim(tokens, start, GROUP, 0)
        gate_rows = lax.dynamic_slice_in_dim(gate_grad, start, GROUP, 0)
        up_rows = lax.dynamic_slice_in_dim(up_grad, start, GROUP, 0)
        hidden_rows = lax.dynamic_slice_in_dim(hidden, start, GROUP, 0)
        grad_rows = lax.dynamic_slice_in_dim(rows_grad, start, GROUP, 0)
        term = jnp.stack([
            jnp.dot(gate_rows.T, rows, preferred_element_type=jnp.float32),
            jnp.dot(up_rows.T, rows, preferred_element_type=jnp.float32),
            jnp.dot(hidden_rows.T, grad_rows, preferred_element_type=jnp.float32)])
        return carry + rounded(term), None

    total, unused_two = lax.scan(group_sums, jnp.zeros((3, FF, D), jnp.float32), jnp.arange(N_DP, dtype=jnp.int32))
    weight_grad = total.astype(jnp.bfloat16)
    return mixed, token_grad, weight_grad
```

```python
import functools

import jax
import jax.numpy as jnp
from jax import lax
from jax.experimental import pallas as pl
from jax.experimental.pallas import tpu as pltpu
from jax.sharding import PartitionSpec as P

MESH = pl.DeviceIdType.MESH
F32 = jnp.float32
BF16 = jnp.bfloat16

SIZES = (4, 6, 8)
HOP = 2


def kernel(
    sizes, tok_ref, og_ref, gate_ref, mask_ref, w_hbm, mixed_ref, tgrad_ref, wgrad_ref,
    xs, xr, G, TR, W, HT, HR, TERM, SIB, SB, RB, ZS, ZR, DW, SZ, RZ,
    w_sem, xs_s, xs_r, az_s, az_r, ag_s, ag_r, sib_s, sib_r, t_s, t_r, tf_s, tf_r,
    h_s, h_r, ts_s, ts_r, rs_s, rs_r, rz_s, rz_r, fs_s, fs_r, z_s, z_r,
):
    NX, NZ, NY = sizes
    NK = NY // 2
    D = tok_ref.shape[1]
    F = W.shape[1]
    FP = HT.shape[1] // 3
    T = G.shape[1]
    HALF = D // 2
    XC = D // NX
    ZROWS = NY * 16

    dp = lax.axis_index("dp")
    ex = lax.axis_index("expert")
    x, q = dp // NZ, dp % NZ
    zh, y, c = ex // (2 * NY), (ex // 2) % NY, ex % 2
    oc, oz = 1 - c, 1 - zh
    zhp = (zh, oz)

    def at(x=x, q=q, zh=zh, y=y, c=c):
        return (x * NZ + q, zh * (2 * NY) + y * 2 + c)

    def remote(src, dst, ss, rs, to):
        return pltpu.make_async_remote_copy(
            src_ref=src, dst_ref=dst, send_sem=ss, recv_sem=rs, device_id=to, device_id_type=MESH
        )

    sibling = at(c=oc)
    zpartner = at(zh=oz)
    ynext = (at(y=(y + 1) % NY), at(y=(y + NY - 1) % NY))
    xnext = [at(x=(x + r) % NX) for r in range(1, NX)]
    znext = (at(q=(q + 1) % NZ), at(q=(q + NZ - 1) % NZ))

    w_copy = pltpu.make_async_copy(w_hbm, W, w_sem)
    w_copy.start()

    barrier = pltpu.get_barrier_semaphore()
    partners = [sibling, zpartner, *ynext, *xnext, *znext]
    for p in partners:
        pl.semaphore_signal(barrier, inc=1, device_id=p, device_id_type=MESH)

    tok = tok_ref[...].astype(F32)
    combine = gate_ref[:, 0:1]
    rg = (combine * og_ref[...].astype(F32)).astype(BF16).astype(F32)
    xs[...] = jnp.where(c == 0, rg, tok)
    pl.semaphore_wait(barrier, len(partners))

    swap = remote(xs, xr, xs_s, xs_r, sibling)
    swap.start()
    swap.wait()
    got = xr[...]
    own = jnp.where(c == 0, tok, rg)
    block = jnp.concatenate([jnp.where(c == 0, own, got), jnp.where(c == 0, got, own)], axis=0)

    def rows_of(zhv, yv, n=16):
        return pl.ds(pl.multiple_of((zhv * NY + yv) * 16, 16), n)

    def half_of(h):
        return pl.ds(h * HALF, HALF)

    my_rows = rows_of(zh, y)
    G[c, my_rows, :] = block.astype(BF16)

    def sgn(dr):
        return 1 if dr == 0 else -1

    def ag_copy(ph, dr, k, h, origin):
        ref = G.at[c, rows_of(zhp[ph], origin), half_of(h)]
        return remote(ref, ref, ag_s.at[ph, dr, k - 1, h], ag_r.at[ph, dr, k - 1, h], ynext[dr])

    started = []

    def ag_send(ph, dr, k, h):
        cp = ag_copy(ph, dr, k, h, (y + 2 * NY - sgn(dr) * (k - 1)) % NY)
        cp.start()
        started.append(cp)

    def spread(ph, origin):
        rows = rows_of(zhp[ph], origin)
        ref = G.at[c, rows, :]
        remote(ref, ref, sib_s.at[ph], sib_r.at[ph], sibling).start()
        for r in range(1, NX):
            cols = pl.ds(pl.multiple_of(((x + r) % NX) * XC, 128), XC)
            remote(
                G.at[c, rows, cols], TR.at[c, r - 1, rows, :],
                t_s.at[r - 1, ph], t_r.at[r - 1, ph], xnext[r - 1],
            ).start()

    def ag_has(dr, k, h):
        return k < NK or h == dr

    def ag_first(ph):
        for h in range(2):
            for dr in range(2):
                if ag_has(dr, 1, h):
                    ag_send(ph, dr, 1, h)
        spread(ph, y)

    def ag_step(ph, k):
        for h in range(2):
            for dr in range(2):
                if not ag_has(dr, k, h):
                    continue
                origin = (y + 2 * NY - sgn(dr) * k) % NY
                ag_copy(ph, dr, k, h, origin).wait_recv()
                if k < NK and ag_has(dr, k + 1, h):
                    ag_send(ph, dr, k + 1, h)
        spread(ph, (y + NY - k) % NY)
        if k < NK:
            spread(ph, (y + k) % NY)

    az = remote(G.at[c, my_rows, :], G.at[c, my_rows, :], az_s, az_r, zpartner)
    az.start()
    ag_first(0)
    order = [(0, k) for k in range(1, NK // 2 + 1)] + [(1, 0)]
    late0 = [(0, k) for k in range(NK // 2 + 1, NK + 1)]
    late1 = [(1, k) for k in range(1, NK + 1)]
    while late0 or late1:
        if late0:
            order.append(late0.pop(0))
        if late1:
            order.append(late1.pop(0))
    for ph, k in order:
        if k == 0:
            there = G.at[c, rows_of(oz, y), :]
            remote(there, there, az_s, az_r, zpartner).wait_recv()
            ag_first(1)
        else:
            ag_step(ph, k)
    w_copy.wait()
    for ph in range(2):
        ref = G.at[oc, rows_of(zhp[ph], 0, ZROWS), :]
        remote(ref, ref, sib_s.at[ph], sib_r.at[ph], sibling).wait_recv()

    def contract(m, a):
        def step(i, acc):
            cols = pl.ds(pl.multiple_of(i * XC, 128), XC)
            return acc + lax.dot_general(
                W[m, :, cols], G[a, :, cols], (((1,), (1,)), ((), ())), preferred_element_type=F32
            )
        return lax.fori_loop(0, NX, step, jnp.zeros((F, T), F32))

    pre_gate, pre_up, back = contract(0, 0), contract(1, 0), contract(2, 1)
    lane = lax.broadcasted_iota(jnp.int32, (1, T), 1)
    live = jnp.where(lane < T // 2, mask_ref[0], mask_ref[1]).astype(F32)
    sig = jax.nn.sigmoid(pre_gate)
    silu = pre_gate * sig
    hidden = live * silu * pre_up
    gate_grad = live * back * pre_up * (sig * (1.0 + pre_gate * (1.0 - sig)))
    up_grad = live * back * silu
    pad = jnp.zeros((FP - F, T), F32)
    h_copies = []
    for m, v in enumerate((gate_grad, up_grad, hidden)):
        HT[0, m * FP:(m + 1) * FP, :] = jnp.concatenate([v, pad], axis=0).astype(BF16)
        for r in range(1, NX):
            cp = remote(
                HT.at[0, pl.ds(m * FP, FP), :], HT.at[r, pl.ds(m * FP, FP), :],
                h_s.at[m, r - 1], h_r.at[m, r - 1], xnext[r - 1],
            )
            cp.start()
            h_copies.append(cp)
        HR[m] = v.T.astype(BF16)

    def terms(ph):
        rows = rows_of(zhp[ph], 0, ZROWS)

        def step(i, carry):
            cols = pl.ds(pl.multiple_of(i * XC, 128), XC)
            dot = functools.partial(jnp.dot, preferred_element_type=F32)
            TERM[0, rows, cols] = dot(HR[2, rows, :], W[2, :, cols]).astype(BF16)
            TERM[1, rows, cols] = (
                dot(HR[0, rows, :], W[0, :, cols]) + dot(HR[1, rows, :], W[1, :, cols])
            ).astype(BF16)
            return carry

        lax.fori_loop(0, NX, step, 0)
        cp = remote(TERM.at[oc, rows, :], SIB.at[rows, :], ts_s.at[ph], ts_r.at[ph], sibling)
        cp.start()
        started.append(cp)
        return cp

    term_copies = {ph: terms(ph) for ph in (1, 0)}

    def t_copy(a, r, ph, ss, rs):
        ref = TR.at[a, r - 1, rows_of(zhp[ph], 0, ZROWS), :]
        return remote(ref, ref, ss.at[r - 1, ph], rs.at[r - 1, ph], sibling)

    for ph in range(2):
        for r in range(1, NX):
            t_copy(c, r, ph, t_s, t_r).wait_recv()
            cp = t_copy(c, r, ph, tf_s, tf_r)
            cp.start()
            started.append(cp)

    def shares(ph, yv, h):
        rows = rows_of(zhp[ph], yv)
        return TERM[c, rows, half_of(h)].astype(F32) + SIB[rows, half_of(h)].astype(F32)

    def rs_has(dr, k, h):
        return k >= 1 and (k > 1 or h == dr)

    def rs_copy(ph, dr, k, h):
        return remote(
            SB.at[ph, dr, k - 1, h], RB.at[ph, dr, k - 1, h],
            rs_s.at[ph, dr, k - 1, h], rs_r.at[ph, dr, k - 1, h], ynext[dr],
        )

    def rs_send(ph, dr, k, h):
        value = shares(ph, (y + 2 * NY + sgn(dr) * (NK + 1 - k)) % NY, h)
        if rs_has(dr, k - 1, h):
            rs_copy(ph, dr, k - 1, h).wait_recv()
            value = value + RB[ph, dr, k - 2, h].astype(F32)
        SB[ph, dr, k - 1, h] = value.astype(BF16)
        cp = rs_copy(ph, dr, k, h)
        cp.start()
        started.append(cp)

    def rs_open(ph):
        term_copies[ph].wait_recv()
        for dr in range(2):
            rs_send(ph, dr, 1, dr)
        for dr in range(2):
            rs_send(ph, dr, 2, 1 - dr)

    def rs_step(ph, k):
        for h in range(2):
            for dr in range(2):
                if k > 2 or h == dr:
                    rs_send(ph, dr, k, h)

    def rs_total(ph):
        parts = []
        for h in range(2):
            value = shares(ph, y, h)
            for dr in range(2):
                if rs_has(dr, NK, h):
                    rs_copy(ph, dr, NK, h).wait_recv()
                    value = value + RB[ph, dr, NK - 1, h].astype(F32)
            parts.append(value)
        return jnp.concatenate(parts, axis=1)

    rz = remote(ZS, ZR, rz_s, rz_r, zpartner)

    def rs_partner():
        ZS[...] = rs_total(1).astype(BF16)
        rz.start()

    final = remote(xs, xr, fs_s, fs_r, sibling)

    def rs_own():
        total = rs_total(0)
        rz.wait_recv()
        total = total + ZR[...].astype(F32)
        first, second = total[0:8, :], total[8:16, :]
        xs[...] = jnp.where(c == 0, second, first)
        final.start()
        final.wait()
        mine = jnp.where(c == 0, first, second)
        other = xr[...]
        mixed_ref[...] = (combine * jnp.where(c == 0, mine, other)).astype(BF16)
        tgrad_ref[...] = jnp.where(c == 0, other, mine).astype(BF16)

    def weight_part(m):
        a = 0 if m < 2 else 1
        if m == 0:
            for ph in range(2):
                for r in range(1, NX):
                    t_copy(oc, r, ph, tf_s, tf_r).wait_recv()
        total = jnp.dot(
            HT[0, m * FP:(m + 1) * FP, :], G[a, :, pl.ds(pl.multiple_of(x * XC, 128), XC)],
            preferred_element_type=F32,
        )
        for r in range(1, NX):
            h_copies[m * (NX - 1) + r - 1].wait_recv()
            total = total + jnp.dot(
                HT[r, m * FP:(m + 1) * FP, :], TR[a, r - 1], preferred_element_type=F32
            )
        for d in range(NZ):
            DW[m, d] = total[:, d * 128:(d + 1) * 128]

    n = NZ - 1

    def z_copy(dr, m, d):
        return remote(
            SZ.at[dr, m, d], RZ.at[dr, m, d], z_s.at[dr, m, d], z_r.at[dr, m, d], znext[dr]
        )

    def z_sends(dr, d):
        return q < d if dr == 0 else q > d

    def z_gets(dr):
        return q > 0 if dr == 0 else q < NZ - 1

    def z_slot(slot, carry):
        for dr in range(2):
            i = slot - HOP * (q if dr == 0 else NZ - 1 - q)
            m, j = jnp.maximum(i, 0) // n, jnp.maximum(i, 0) % n
            d = NZ - 1 - j if dr == 0 else j

            @pl.when((i >= 0) & (i < 3 * n) & z_sends(dr, d))
            def _():
                @pl.when(z_gets(dr))
                def _():
                    z_copy(dr, m, d).wait_recv()
                value = DW[m, d] + jnp.where(z_gets(dr), RZ[dr, m, d].astype(F32), 0.0)
                SZ[dr, m, d] = value.astype(BF16)
                z_copy(dr, m, d).start()
        return carry

    slots = 3 * n + HOP * n
    marks = {}
    rs_open(1)
    rs_open(0)
    later = [functools.partial(rs_step, ph, k) for k in range(2, NK + 1) for ph in (1, 0)]
    later += [rs_partner]
    for i, f in enumerate(later):
        marks.setdefault(min(2 + 2 * i, slots - 1), []).append(f)
    begin = 0
    for slot in range(slots + 1):
        here = marks.get(slot, [])
        dw = slot % n == 0 and slot // n < 3
        if (here or dw or slot == slots) and slot > begin:
            lax.fori_loop(begin, slot, z_slot, 0)
            begin = slot
        if dw:
            weight_part(slot // n)
        for f in here:
            f()
    rs_own()
    for m in range(3):
        value = DW[m, q]
        for dr in range(2):
            @pl.when(z_gets(dr))
            def _():
                z_copy(dr, m, q).wait_recv()
            value = value + jnp.where(z_gets(dr), RZ[dr, m, q].astype(F32), 0.0)
        wgrad_ref[m] = value[:F, :].astype(BF16)

    for cp in started:
        cp.wait_send()
    for cp in h_copies:
        cp.wait_send()
    az.wait_send()
    rz.wait_send()
    for ph in range(2):
        ref = G.at[c, rows_of(zhp[ph], 0, ZROWS), :]
        remote(ref, ref, sib_s.at[ph], sib_r.at[ph], sibling).wait_send()
        for r in range(1, NX):
            t_copy(c, r, ph, t_s, t_r).wait_send()
    for dr in range(2):
        def drain(i, carry):
            m, d = i // NZ, i % NZ

            @pl.when(z_sends(dr, d))
            def _():
                z_copy(dr, m, d).wait_send()
            return carry
        lax.fori_loop(0, 3 * NZ, drain, 0)


def body(sizes, tokens, row_gate, block_mask, weights, out_grad):
    NX, NZ, NY = sizes
    NK = NY // 2
    D = tokens.shape[1]
    F = weights.shape[1]
    FP = -(-F // 16) * 16
    T = NY * 32
    gate = jnp.broadcast_to(row_gate.astype(F32)[:, None], (8, 128))
    vmem = pl.BlockSpec(memory_space=pltpu.VMEM)
    dma = pltpu.SemaphoreType.DMA
    V = pltpu.VMEM
    return pl.pallas_call(
        functools.partial(kernel, sizes),
        out_shape=(
            jax.ShapeDtypeStruct((8, D), BF16),
            jax.ShapeDtypeStruct((8, D), BF16),
            jax.ShapeDtypeStruct((3, F, 128), BF16),
        ),
        in_specs=[vmem, vmem, vmem, pl.BlockSpec(memory_space=pltpu.SMEM), pl.BlockSpec(memory_space=pl.ANY)],
        out_specs=(vmem, vmem, vmem),
        scratch_shapes=[
            V((8, D), F32), V((8, D), F32),
            V((2, T, D), BF16),
            V((2, NX - 1, T, D // NX), BF16),
            V((3, F, D), BF16),
            V((NX, 3 * FP, T), BF16),
            V((3, T, F), BF16),
            V((2, T, D), BF16), V((T, D), BF16),
            V((2, 2, NK, 2, 16, D // 2), BF16), V((2, 2, NK, 2, 16, D // 2), BF16),
            V((16, D), BF16), V((16, D), BF16),
            V((3, NZ, FP, 128), F32),
            V((2, 3, NZ, FP, 128), BF16), V((2, 3, NZ, FP, 128), BF16),
            dma, dma, dma, dma, dma,
            dma((2, 2, NK, 2)), dma((2, 2, NK, 2)),
            dma((2,)), dma((2,)),
            dma((NX - 1, 2)), dma((NX - 1, 2)),
            dma((NX - 1, 2)), dma((NX - 1, 2)),
            dma((3, NX - 1)), dma((3, NX - 1)),
            dma((2,)), dma((2,)),
            dma((2, 2, NK, 2)), dma((2, 2, NK, 2)),
            dma, dma, dma, dma,
            dma((2, 3, NZ)), dma((2, 3, NZ)),
        ],
        compiler_params=pltpu.CompilerParams(
            collective_id=0, has_side_effects=True, vmem_limit_bytes=48 << 20
        ),
        cost_estimate=pl.CostEstimate(flops=9 * 2 * T * D * F, bytes_accessed=8 * D * F, transcendentals=T * F),
    )(tokens, out_grad, gate, block_mask, weights)


def solution(mesh):
    in_specs = (
        P(("dp", "expert"), None),
        P(("dp", "expert")),
        P("dp"),
        P(None, "expert", None),
        P(("dp", "expert"), None),
    )
    out_specs = (P(("dp", "expert"), None), P(("dp", "expert"), None), P(None, "expert", "dp"))
    return jax.shard_map(
        functools.partial(body, SIZES), mesh=mesh, in_specs=in_specs, out_specs=out_specs, check_vma=False
    )
```

```python
import functools

import jax
import jax.numpy as jnp
from jax import lax
from jax.experimental import pallas as pl
from jax.experimental.pallas import tpu as pltpu
from jax.sharding import PartitionSpec as P

MESH = pl.DeviceIdType.MESH
F32 = jnp.float32
BF16 = jnp.bfloat16

SIZES = (4, 6, 8)
HOP = 3
FIRST = (0, 2, 4)
EARLY = True


def kernel(
    sizes, tok_ref, og_ref, gate_ref, mask_ref, w_hbm, mixed_ref, tgrad_ref, wgrad_ref,
    xs, xr, G, TR, W, HT, HR, TERM, SIB, SB, RB, ZS, ZR, DW, SZ, RZ,
    w_sem, xs_s, xs_r, az_s, az_r, ag_s, ag_r, sib_s, sib_r, t_s, t_r, tf_s, tf_r,
    h_s, h_r, ts_s, ts_r, rs_s, rs_r, rz_s, rz_r, fs_s, fs_r, z_s, z_r,
):
    NX, NZ, NY = sizes
    NK = NY // 2
    D = tok_ref.shape[1]
    F = W.shape[1]
    FP = HT.shape[1] // 3
    T = G.shape[1]
    HALF = D // 2
    XC = D // NX
    ZROWS = NY * 16

    dp = lax.axis_index("dp")
    ex = lax.axis_index("expert")
    x, q = dp // NZ, dp % NZ
    zh, y, c = ex // (2 * NY), (ex // 2) % NY, ex % 2
    oc, oz = 1 - c, 1 - zh
    zhp = (zh, oz)

    def at(x=x, q=q, zh=zh, y=y, c=c):
        return (x * NZ + q, zh * (2 * NY) + y * 2 + c)

    def remote(src, dst, ss, rs, to):
        return pltpu.make_async_remote_copy(
            src_ref=src, dst_ref=dst, send_sem=ss, recv_sem=rs, device_id=to, device_id_type=MESH
        )

    sibling = at(c=oc)
    zpartner = at(zh=oz)
    ynext = (at(y=(y + 1) % NY), at(y=(y + NY - 1) % NY))
    xnext = [at(x=(x + r) % NX) for r in range(1, NX)]
    znext = (at(q=(q + 1) % NZ), at(q=(q + NZ - 1) % NZ))

    w_copy = pltpu.make_async_copy(w_hbm, W, w_sem)
    w_copy.start()

    barrier = pltpu.get_barrier_semaphore()
    partners = [sibling, zpartner, *ynext, *xnext, *znext]
    for p in partners:
        pl.semaphore_signal(barrier, inc=1, device_id=p, device_id_type=MESH)

    tok = tok_ref[...].astype(F32)
    combine = gate_ref[:, 0:1]
    rg = (combine * og_ref[...].astype(F32)).astype(BF16).astype(F32)
    xs[...] = jnp.where(c == 0, rg, tok)
    pl.semaphore_wait(barrier, len(partners))

    swap = remote(xs, xr, xs_s, xs_r, sibling)
    swap.start()
    swap.wait()
    got = xr[...]
    own = jnp.where(c == 0, tok, rg)
    block = jnp.concatenate([jnp.where(c == 0, own, got), jnp.where(c == 0, got, own)], axis=0)

    def rows_of(zhv, yv, n=16):
        return pl.ds(pl.multiple_of((zhv * NY + yv) * 16, 16), n)

    def half_of(h):
        return pl.ds(h * HALF, HALF)

    my_rows = rows_of(zh, y)
    G[c, my_rows, :] = block.astype(BF16)

    def sgn(dr):
        return 1 if dr == 0 else -1

    def ag_copy(ph, dr, k, h, origin):
        ref = G.at[c, rows_of(zhp[ph], origin), half_of(h)]
        return remote(ref, ref, ag_s.at[ph, dr, k - 1, h], ag_r.at[ph, dr, k - 1, h], ynext[dr])

    started = []

    def ag_send(ph, dr, k, h):
        cp = ag_copy(ph, dr, k, h, (y + 2 * NY - sgn(dr) * (k - 1)) % NY)
        cp.start()
        started.append(cp)

    def spread(ph, origin):
        rows = rows_of(zhp[ph], origin)
        ref = G.at[c, rows, :]
        remote(ref, ref, sib_s.at[ph], sib_r.at[ph], sibling).start()
        for r in range(1, NX):
            cols = pl.ds(pl.multiple_of(((x + r) % NX) * XC, 128), XC)
            remote(
                G.at[c, rows, cols], TR.at[c, r - 1, rows, :],
                t_s.at[r - 1, ph], t_r.at[r - 1, ph], xnext[r - 1],
            ).start()

    def ag_has(dr, k, h):
        return k < NK or h == dr

    def ag_first(ph):
        for h in range(2):
            if ph == 1:
                az_copy(rows_of(oz, y), h).wait_recv()
            for dr in range(2):
                if ag_has(dr, 1, h):
                    ag_send(ph, dr, 1, h)
        spread(ph, y)

    def ag_step(ph, k):
        for h in range(2):
            for dr in range(2):
                if not ag_has(dr, k, h):
                    continue
                origin = (y + 2 * NY - sgn(dr) * k) % NY
                ag_copy(ph, dr, k, h, origin).wait_recv()
                if k < NK and ag_has(dr, k + 1, h):
                    ag_send(ph, dr, k + 1, h)
        spread(ph, (y + NY - k) % NY)
        if k < NK:
            spread(ph, (y + k) % NY)

    def az_copy(rows, h):
        ref = G.at[c, rows, half_of(h)]
        return remote(ref, ref, az_s.at[h], az_r.at[h], zpartner)

    for h in range(2):
        cp = az_copy(my_rows, h)
        cp.start()
        started.append(cp)

    def contract(m, a, ph):
        rows = rows_of(zhp[ph], 0, ZROWS)

        def step(i, acc):
            cols = pl.ds(pl.multiple_of(i * XC, 128), XC)
            return acc + lax.dot_general(
                W[m, :, cols], G[a, rows, cols], (((1,), (1,)), ((), ())), preferred_element_type=F32
            )
        return lax.fori_loop(0, NX, step, jnp.zeros((F, ZROWS), F32))

    def h_copy(ph, m, r):
        spot = (pl.ds(m * FP, FP), pl.ds(pl.multiple_of(zhp[ph] * ZROWS, ZROWS), ZROWS))
        return remote(
            HT.at[0, *spot], HT.at[r, *spot], h_s.at[ph, m, r - 1], h_r.at[ph, m, r - 1], xnext[r - 1]
        )

    held = {}

    def hidden_first(ph):
        ref = G.at[oc, rows_of(zhp[ph], 0, ZROWS), :]
        remote(ref, ref, sib_s.at[ph], sib_r.at[ph], sibling).wait_recv()
        if ph == 0:
            w_copy.wait()
        held[ph] = contract(0, 0, ph), contract(1, 0, ph)

    def hidden_second(ph):
        pre_gate, pre_up = held[ph]
        back = contract(2, 1, ph)
        live = mask_ref[zhp[ph]].astype(F32)
        sig = jax.nn.sigmoid(pre_gate)
        silu = pre_gate * sig
        hidden = live * silu * pre_up
        gate_grad = live * back * pre_up * (sig * (1.0 + pre_gate * (1.0 - sig)))
        up_grad = live * back * silu
        pad = jnp.zeros((FP - F, ZROWS), F32)
        lanes = pl.ds(pl.multiple_of(zhp[ph] * ZROWS, ZROWS), ZROWS)
        for m, v in enumerate((gate_grad, up_grad, hidden)):
            HT[0, m * FP:(m + 1) * FP, lanes] = jnp.concatenate([v, pad], axis=0).astype(BF16)
            for r in range(1, NX):
                h_copy(ph, m, r).start()
        for m, v in enumerate((gate_grad, up_grad, hidden)):
            HR[m, rows_of(zhp[ph], 0, ZROWS), :] = v.T.astype(BF16)

    ag_first(0)
    late0 = [(0, k) for k in range(NK // 2 + 1, NK + 1)]
    late1 = [(1, k) for k in range(1, NK + 1)]
    order = [(0, k) for k in range(1, NK // 2 + 1)] + [(1, 0)]
    while late0 or late1:
        if late0:
            order.append(late0.pop(0))
        if late1:
            order.append(late1.pop(0))
    work = [functools.partial(hidden_first, 0), functools.partial(hidden_second, 0)]
    for ph, k in order:
        if k == 0:
            ag_first(1)
        else:
            ag_step(ph, k)
        if EARLY and ph == 1 and k >= NK - 2 and work:
            work.pop(0)()
    work += [functools.partial(hidden_first, 1), functools.partial(hidden_second, 1)]
    for f in work:
        f()

    def terms(ph):
        rows = rows_of(zhp[ph], 0, ZROWS)

        def step(i, carry):
            cols = pl.ds(pl.multiple_of(i * XC, 128), XC)
            dot = functools.partial(jnp.dot, preferred_element_type=F32)
            TERM[0, rows, cols] = dot(HR[2, rows, :], W[2, :, cols]).astype(BF16)
            TERM[1, rows, cols] = (
                dot(HR[0, rows, :], W[0, :, cols]) + dot(HR[1, rows, :], W[1, :, cols])
            ).astype(BF16)
            return carry

        lax.fori_loop(0, NX, step, 0)
        cp = remote(TERM.at[oc, rows, :], SIB.at[rows, :], ts_s.at[ph], ts_r.at[ph], sibling)
        cp.start()
        started.append(cp)
        return cp

    term_copies = {ph: terms(ph) for ph in (1, 0)}

    def t_copy(a, r, ph, ss, rs):
        ref = TR.at[a, r - 1, rows_of(zhp[ph], 0, ZROWS), :]
        return remote(ref, ref, ss.at[r - 1, ph], rs.at[r - 1, ph], sibling)

    for ph in range(2):
        for r in range(1, NX):
            t_copy(c, r, ph, t_s, t_r).wait_recv()
            cp = t_copy(c, r, ph, tf_s, tf_r)
            cp.start()
            started.append(cp)

    def shares(ph, yv, h):
        rows = rows_of(zhp[ph], yv)
        return TERM[c, rows, half_of(h)].astype(F32) + SIB[rows, half_of(h)].astype(F32)

    def rs_has(dr, k, h):
        return k >= 1 and (k > 1 or h == dr)

    def rs_copy(ph, dr, k, h):
        return remote(
            SB.at[ph, dr, k - 1, h], RB.at[ph, dr, k - 1, h],
            rs_s.at[ph, dr, k - 1, h], rs_r.at[ph, dr, k - 1, h], ynext[dr],
        )

    def rs_send(ph, dr, k, h):
        value = shares(ph, (y + 2 * NY + sgn(dr) * (NK + 1 - k)) % NY, h)
        if rs_has(dr, k - 1, h):
            rs_copy(ph, dr, k - 1, h).wait_recv()
            value = value + RB[ph, dr, k - 2, h].astype(F32)
        SB[ph, dr, k - 1, h] = value.astype(BF16)
        cp = rs_copy(ph, dr, k, h)
        cp.start()
        started.append(cp)

    def rs_open(ph):
        term_copies[ph].wait_recv()
        for dr in range(2):
            rs_send(ph, dr, 1, dr)
        for dr in range(2):
            rs_send(ph, dr, 2, 1 - dr)

    def rs_step(ph, k):
        for h in range(2):
            for dr in range(2):
                if k > 2 or h == dr:
                    rs_send(ph, dr, k, h)

    def rs_total(ph):
        parts = []
        for h in range(2):
            value = shares(ph, y, h)
            for dr in range(2):
                if rs_has(dr, NK, h):
                    rs_copy(ph, dr, NK, h).wait_recv()
                    value = value + RB[ph, dr, NK - 1, h].astype(F32)
            parts.append(value)
        return jnp.concatenate(parts, axis=1)

    rz = remote(ZS, ZR, rz_s, rz_r, zpartner)

    def rs_partner():
        ZS[...] = rs_total(1).astype(BF16)
        rz.start()

    final = remote(xs, xr, fs_s, fs_r, sibling)

    def rs_own():
        total = rs_total(0)
        rz.wait_recv()
        total = total + ZR[...].astype(F32)
        first, second = total[0:8, :], total[8:16, :]
        xs[...] = jnp.where(c == 0, second, first)
        final.start()
        final.wait()
        mine = jnp.where(c == 0, first, second)
        other = xr[...]
        mixed_ref[...] = (combine * jnp.where(c == 0, mine, other)).astype(BF16)
        tgrad_ref[...] = jnp.where(c == 0, other, mine).astype(BF16)

    def weight_part(m):
        a = 0 if m < 2 else 1
        if m == 0:
            for ph in range(2):
                for r in range(1, NX):
                    t_copy(oc, r, ph, tf_s, tf_r).wait_recv()
        total = jnp.dot(
            HT[0, m * FP:(m + 1) * FP, :], G[a, :, pl.ds(pl.multiple_of(x * XC, 128), XC)],
            preferred_element_type=F32,
        )
        for r in range(1, NX):
            for ph in range(2):
                h_copy(ph, m, r).wait_recv()
            total = total + jnp.dot(
                HT[r, m * FP:(m + 1) * FP, :], TR[a, r - 1], preferred_element_type=F32
            )
        for d in range(NZ):
            DW[m, d] = total[:, d * 128:(d + 1) * 128]

    n = NZ - 1

    def z_copy(dr, m, d):
        return remote(
            SZ.at[dr, m, d], RZ.at[dr, m, d], z_s.at[dr, m, d], z_r.at[dr, m, d], znext[dr]
        )

    def z_sends(dr, d):
        return q < d if dr == 0 else q > d

    def z_gets(dr):
        return q > 0 if dr == 0 else q < NZ - 1

    left = {m: 0 for m in range(3)}
    stream = []
    for i in range(3 * n):
        ready = [m for m in range(3) if left[m] < n and (FIRST[m] <= i or m == 0)]
        ready = ready or [m for m in range(3) if left[m] < n]
        m = min(ready, key=lambda m: (left[m], m))
        stream.append((m, left[m]))
        left[m] += 1
    first_use = [min(i for i, v in enumerate(stream) if v[0] == m) for m in range(3)]

    def looked_up(i, which):
        value = jnp.int32(0)
        for k, v in enumerate(stream):
            if v[which]:
                value = jnp.where(i == k, v[which], value)
        return value

    def z_slot(slot, carry):
        for dr in range(2):
            i = slot - HOP * (q if dr == 0 else NZ - 1 - q)
            m, j = looked_up(i, 0), looked_up(i, 1)
            d = NZ - 1 - j if dr == 0 else j

            @pl.when((i >= 0) & (i < 3 * n) & z_sends(dr, d))
            def _():
                @pl.when(z_gets(dr))
                def _():
                    z_copy(dr, m, d).wait_recv()
                value = DW[m, d] + jnp.where(z_gets(dr), RZ[dr, m, d].astype(F32), 0.0)
                SZ[dr, m, d] = value.astype(BF16)
                z_copy(dr, m, d).start()
        return carry

    slots = 3 * n + HOP * n
    marks = {}
    rs_open(1)
    rs_open(0)
    later = [functools.partial(rs_step, ph, k) for k in range(2, NK + 1) for ph in (1, 0)]
    later += [rs_partner]
    for i, f in enumerate(later):
        marks.setdefault(min(2 + 2 * i, slots - 1), []).append(f)
    begin = 0
    for slot in range(slots + 1):
        here = marks.get(slot, [])
        dw = slot in first_use
        if (here or dw or slot == slots) and slot > begin:
            lax.fori_loop(begin, slot, z_slot, 0)
            begin = slot
        if dw:
            weight_part(first_use.index(slot))
        for f in here:
            f()
    rs_own()
    for m in range(3):
        value = DW[m, q]
        for dr in range(2):
            @pl.when(z_gets(dr))
            def _():
                z_copy(dr, m, q).wait_recv()
            value = value + jnp.where(z_gets(dr), RZ[dr, m, q].astype(F32), 0.0)
        wgrad_ref[m] = value[:F, :].astype(BF16)

    for cp in started:
        cp.wait_send()
    for ph in range(2):
        for m in range(3):
            for r in range(1, NX):
                h_copy(ph, m, r).wait_send()
    rz.wait_send()
    for ph in range(2):
        ref = G.at[c, rows_of(zhp[ph], 0, ZROWS), :]
        remote(ref, ref, sib_s.at[ph], sib_r.at[ph], sibling).wait_send()
        for r in range(1, NX):
            t_copy(c, r, ph, t_s, t_r).wait_send()
    for dr in range(2):
        def drain(i, carry):
            m, d = i // NZ, i % NZ

            @pl.when(z_sends(dr, d))
            def _():
                z_copy(dr, m, d).wait_send()
            return carry
        lax.fori_loop(0, 3 * NZ, drain, 0)


def body(sizes, tokens, row_gate, block_mask, weights, out_grad):
    NX, NZ, NY = sizes
    NK = NY // 2
    D = tokens.shape[1]
    F = weights.shape[1]
    FP = -(-F // 16) * 16
    T = NY * 32
    gate = jnp.broadcast_to(row_gate.astype(F32)[:, None], (8, 128))
    vmem = pl.BlockSpec(memory_space=pltpu.VMEM)
    dma = pltpu.SemaphoreType.DMA
    V = pltpu.VMEM
    return pl.pallas_call(
        functools.partial(kernel, sizes),
        out_shape=(
            jax.ShapeDtypeStruct((8, D), BF16),
            jax.ShapeDtypeStruct((8, D), BF16),
            jax.ShapeDtypeStruct((3, F, 128), BF16),
        ),
        in_specs=[vmem, vmem, vmem, pl.BlockSpec(memory_space=pltpu.SMEM), pl.BlockSpec(memory_space=pl.ANY)],
        out_specs=(vmem, vmem, vmem),
        scratch_shapes=[
            V((8, D), F32), V((8, D), F32),
            V((2, T, D), BF16),
            V((2, NX - 1, T, D // NX), BF16),
            V((3, F, D), BF16),
            V((NX, 3 * FP, T), BF16),
            V((3, T, F), BF16),
            V((2, T, D), BF16), V((T, D), BF16),
            V((2, 2, NK, 2, 16, D // 2), BF16), V((2, 2, NK, 2, 16, D // 2), BF16),
            V((16, D), BF16), V((16, D), BF16),
            V((3, NZ, FP, 128), F32),
            V((2, 3, NZ, FP, 128), BF16), V((2, 3, NZ, FP, 128), BF16),
            dma, dma, dma, dma((2,)), dma((2,)),
            dma((2, 2, NK, 2)), dma((2, 2, NK, 2)),
            dma((2,)), dma((2,)),
            dma((NX - 1, 2)), dma((NX - 1, 2)),
            dma((NX - 1, 2)), dma((NX - 1, 2)),
            dma((2, 3, NX - 1)), dma((2, 3, NX - 1)),
            dma((2,)), dma((2,)),
            dma((2, 2, NK, 2)), dma((2, 2, NK, 2)),
            dma, dma, dma, dma,
            dma((2, 3, NZ)), dma((2, 3, NZ)),
        ],
        compiler_params=pltpu.CompilerParams(
            collective_id=0, has_side_effects=True, vmem_limit_bytes=60 << 20
        ),
        cost_estimate=pl.CostEstimate(flops=9 * 2 * T * D * F, bytes_accessed=8 * D * F, transcendentals=T * F),
    )(tokens, out_grad, gate, block_mask, weights)


def solution(mesh):
    in_specs = (
        P(("dp", "expert"), None),
        P(("dp", "expert")),
        P("dp"),
        P(None, "expert", None),
        P(("dp", "expert"), None),
    )
    out_specs = (P(("dp", "expert"), None), P(("dp", "expert"), None), P(None, "expert", "dp"))
    return jax.shard_map(
        functools.partial(body, SIZES), mesh=mesh, in_specs=in_specs, out_specs=out_specs, check_vma=False
    )
```

```python
import functools

import jax
import jax.numpy as jnp
from jax import lax
from jax.experimental import pallas as pl
from jax.experimental.pallas import tpu as pltpu
from jax.sharding import PartitionSpec as P

MESH = pl.DeviceIdType.MESH
F32 = jnp.float32
BF16 = jnp.bfloat16

SIZES = (4, 6, 8)
HOP = 3
FIRST = (0, 2, 4)
EARLY = True
STEPS = (1, 2, 3)


def kernel(
    sizes, tok_hbm, og_hbm, gate_ref, mask_ref, w_hbm, rows_ref, wgrad_ref,
    xs, xr, G, TR, W, HT, HR, TERM, SIB, SB, RB, ZS, ZR, DW, SZ, RZ,
    in_v, in_sem, w_sem, xs_s, xs_r, az_s, az_r, ag_s, ag_r, sib_s, sib_r, t_s, t_r, tf_s, tf_r,
    h_s, h_r, ts_s, ts_r, rs_s, rs_r, rz_s, rz_r, fs_s, fs_r, z_s, z_r,
):
    NX, NZ, NY = sizes
    NK = NY // 2
    D = tok_hbm.shape[1]
    F = W.shape[1]
    FP = HT.shape[1] // 3
    T = G.shape[1]
    HALF = D // 2
    XC = D // NX
    ZROWS = NY * 16

    dp = lax.axis_index("dp")
    ex = lax.axis_index("expert")
    x, q = dp // NZ, dp % NZ
    zh, y, c = ex // (2 * NY), (ex // 2) % NY, ex % 2
    oc, oz = 1 - c, 1 - zh
    zhp = (zh, oz)

    def at(x=x, q=q, zh=zh, y=y, c=c):
        return (x * NZ + q, zh * (2 * NY) + y * 2 + c)

    def remote(src, dst, ss, rs, to):
        return pltpu.make_async_remote_copy(
            src_ref=src, dst_ref=dst, send_sem=ss, recv_sem=rs, device_id=to, device_id_type=MESH
        )

    sibling = at(c=oc)
    zpartner = at(zh=oz)
    ynext = (at(y=(y + 1) % NY), at(y=(y + NY - 1) % NY))
    xnext = [at(x=(x + r) % NX) for r in range(1, NX)]
    znext = (at(q=(q + 1) % NZ), at(q=(q + NZ - 1) % NZ))

    w_copy = pltpu.make_async_copy(w_hbm, W, w_sem)
    loads = [pltpu.make_async_copy(r, in_v.at[i], in_sem.at[i]) for i, r in enumerate((tok_hbm, og_hbm))]
    for cp in loads:
        cp.start()
    w_copy.start()

    barrier = pltpu.get_barrier_semaphore()
    partners = [sibling, zpartner, *ynext, *xnext, *znext]
    for p in partners:
        pl.semaphore_signal(barrier, inc=1, device_id=p, device_id_type=MESH)

    for cp in loads:
        cp.wait()
    tok = in_v[0].astype(F32)
    spot = (lax.broadcasted_iota(jnp.int32, (8, 8), 0), lax.broadcasted_iota(jnp.int32, (8, 8), 1))
    gates = jnp.broadcast_to(gate_ref[...].astype(F32), (8, 8))
    combine = jnp.sum(jnp.where(spot[0] == spot[1], gates, 0.0), axis=1, keepdims=True)
    rg = (combine * in_v[1].astype(F32)).astype(BF16).astype(F32)
    xs[...] = jnp.where(c == 0, rg, tok)
    pl.semaphore_wait(barrier, len(partners))

    swap = remote(xs, xr, xs_s, xs_r, sibling)
    swap.start()
    swap.wait()
    got = xr[...]
    own = jnp.where(c == 0, tok, rg)
    block = jnp.concatenate([jnp.where(c == 0, own, got), jnp.where(c == 0, got, own)], axis=0)

    def place(o):
        return 0 if o == 0 else (2 * NK - 1 if abs(o) == NK else 2 * abs(o) - (o < 0))

    def rows_at(ph, first, n=1):
        return pl.ds(ph * ZROWS + first * 16, n * 16)

    def rows_of(ph, o):
        return rows_at(ph, place(o))

    def rows_all(ph):
        return pl.ds(ph * ZROWS, ZROWS)

    def half_of(h):
        return pl.ds(h * HALF, HALF)

    G[c, 0:16, :] = block.astype(BF16)

    def sgn(dr):
        return 1 if dr == 0 else -1

    def ag_copy(ph, dr, k, h):
        o = -sgn(dr)
        return remote(
            G.at[c, rows_of(ph, o * (k - 1)), half_of(h)], G.at[c, rows_of(ph, o * k), half_of(h)],
            ag_s.at[ph, dr, k - 1, h], ag_r.at[ph, dr, k - 1, h], ynext[dr],
        )

    started = []

    def ag_send(ph, dr, k, h):
        cp = ag_copy(ph, dr, k, h)
        cp.start()
        started.append(cp)

    def spread(ph, first, n):
        rows = rows_at(ph, first, n)
        ref = G.at[c, rows, :]
        remote(ref, ref, sib_s.at[ph], sib_r.at[ph], sibling).start()
        for r in range(1, NX):
            remote(
                G.at[c, rows, xcols[r]], TR.at[c, r - 1, rows, :],
                t_s.at[r - 1, ph], t_r.at[r - 1, ph], xnext[r - 1],
            ).start()

    xcols = [pl.ds(pl.multiple_of(((x + r) % NX) * XC, 128), XC) for r in range(NX)]

    def ag_has(dr, k, h):
        return k < NK or h == dr

    def az_copy(h):
        return remote(
            G.at[c, rows_of(0, 0), half_of(h)], G.at[c, rows_of(1, 0), half_of(h)], az_s.at[h], az_r.at[h], zpartner
        )

    def ag_first(ph):
        for h in range(2):
            if ph == 1:
                az_copy(h).wait_recv()
            for dr in range(2):
                if ag_has(dr, 1, h):
                    ag_send(ph, dr, 1, h)

    def ag_step(ph, k):
        for h in range(2):
            for dr in range(2):
                if not ag_has(dr, k, h):
                    continue
                ag_copy(ph, dr, k, h).wait_recv()
                if k < NK and ag_has(dr, k + 1, h):
                    ag_send(ph, dr, k + 1, h)
        if (ph, k) in BATCH:
            first, n = BATCH[ph, k]
            spread(ph, first, n)

    BATCH = {}
    for ph in range(2):
        begin = 0
        for k in STEPS:
            if k < NK:
                BATCH[ph, k] = (begin, 2 * k + 1 - begin)
                begin = 2 * k + 1
        BATCH[ph, NK] = (begin, 2 * NK - begin)

    for h in range(2):
        cp = az_copy(h)
        cp.start()
        started.append(cp)

    def contract(m, a, ph):
        rows = rows_all(ph)

        def step(i, acc):
            cols = pl.ds(pl.multiple_of(i * XC, 128), XC)
            return acc + lax.dot_general(
                W[m, :, cols], G[a, rows, cols], (((1,), (1,)), ((), ())), preferred_element_type=F32
            )
        return lax.fori_loop(0, NX, step, jnp.zeros((F, ZROWS), F32))

    def h_copy(ph, m, r):
        spot = (pl.ds(m * FP, FP), rows_all(ph))
        return remote(
            HT.at[0, *spot], HT.at[r, *spot], h_s.at[ph, m, r - 1], h_r.at[ph, m, r - 1], xnext[r - 1]
        )

    held = {}

    def hidden_first(ph):
        ref = G.at[oc, rows_all(ph), :]
        remote(ref, ref, sib_s.at[ph], sib_r.at[ph], sibling).wait_recv()
        if ph == 0:
            w_copy.wait()
        held[ph] = contract(0, 0, ph), contract(1, 0, ph)

    def hidden_second(ph):
        pre_gate, pre_up = held[ph]
        back = contract(2, 1, ph)
        live = mask_ref[zhp[ph]].astype(F32)
        sig = jax.nn.sigmoid(pre_gate)
        silu = pre_gate * sig
        hidden = live * silu * pre_up
        gate_grad = live * back * pre_up * (sig * (1.0 + pre_gate * (1.0 - sig)))
        up_grad = live * back * silu
        pad = jnp.zeros((FP - F, ZROWS), F32)
        lanes = rows_all(ph)
        for m, v in enumerate((gate_grad, up_grad, hidden)):
            HT[0, m * FP:(m + 1) * FP, lanes] = jnp.concatenate([v, pad], axis=0).astype(BF16)
            for r in range(1, NX):
                h_copy(ph, m, r).start()
        for m, v in enumerate((gate_grad, up_grad, hidden)):
            HR[m, rows_all(ph), :] = v.T.astype(BF16)

    ag_first(0)
    late0 = [(0, k) for k in range(NK // 2 + 1, NK + 1)]
    late1 = [(1, k) for k in range(1, NK + 1)]
    order = [(0, k) for k in range(1, NK // 2 + 1)] + [(1, 0)]
    while late0 or late1:
        if late0:
            order.append(late0.pop(0))
        if late1:
            order.append(late1.pop(0))
    work = [functools.partial(hidden_first, 0), functools.partial(hidden_second, 0)]
    for ph, k in order:
        if k == 0:
            ag_first(1)
        else:
            ag_step(ph, k)
        if EARLY and ph == 1 and k >= NK - 2 and work:
            work.pop(0)()
    work += [functools.partial(hidden_first, 1), functools.partial(hidden_second, 1)]
    for f in work:
        f()

    def terms(ph):
        rows = rows_all(ph)

        def step(i, carry):
            cols = pl.ds(pl.multiple_of(i * XC, 128), XC)
            dot = functools.partial(jnp.dot, preferred_element_type=F32)
            TERM[0, rows, cols] = dot(HR[2, rows, :], W[2, :, cols]).astype(BF16)
            TERM[1, rows, cols] = (
                dot(HR[0, rows, :], W[0, :, cols]) + dot(HR[1, rows, :], W[1, :, cols])
            ).astype(BF16)
            return carry

        lax.fori_loop(0, NX, step, 0)
        cp = remote(TERM.at[oc, rows, :], SIB.at[rows, :], ts_s.at[ph], ts_r.at[ph], sibling)
        cp.start()
        started.append(cp)
        return cp

    term_copies = {ph: terms(ph) for ph in (1, 0)}

    def t_copy(a, r, ph, ss, rs):
        ref = TR.at[a, r - 1, rows_all(ph), :]
        return remote(ref, ref, ss.at[r - 1, ph], rs.at[r - 1, ph], sibling)

    for ph in range(2):
        for r in range(1, NX):
            t_copy(c, r, ph, t_s, t_r).wait_recv()
            cp = t_copy(c, r, ph, tf_s, tf_r)
            cp.start()
            started.append(cp)

    def shares(ph, o, h):
        rows = rows_of(ph, o)
        return TERM[c, rows, half_of(h)].astype(F32) + SIB[rows, half_of(h)].astype(F32)

    def rs_has(dr, k, h):
        return k >= 1 and (k > 1 or h == dr)

    def rs_copy(ph, dr, k, h):
        return remote(
            SB.at[ph, dr, k - 1, h], RB.at[ph, dr, k - 1, h],
            rs_s.at[ph, dr, k - 1, h], rs_r.at[ph, dr, k - 1, h], ynext[dr],
        )

    def rs_send(ph, dr, k, h):
        value = shares(ph, sgn(dr) * (NK + 1 - k), h)
        if rs_has(dr, k - 1, h):
            rs_copy(ph, dr, k - 1, h).wait_recv()
            value = value + RB[ph, dr, k - 2, h].astype(F32)
        SB[ph, dr, k - 1, h] = value.astype(BF16)
        cp = rs_copy(ph, dr, k, h)
        cp.start()
        started.append(cp)

    def rs_open(ph):
        term_copies[ph].wait_recv()
        for dr in range(2):
            rs_send(ph, dr, 1, dr)
        for dr in range(2):
            rs_send(ph, dr, 2, 1 - dr)

    def rs_step(ph, k):
        for h in range(2):
            for dr in range(2):
                if k > 2 or h == dr:
                    rs_send(ph, dr, k, h)

    def rs_total(ph):
        parts = []
        for h in range(2):
            value = shares(ph, 0, h)
            for dr in range(2):
                if rs_has(dr, NK, h):
                    rs_copy(ph, dr, NK, h).wait_recv()
                    value = value + RB[ph, dr, NK - 1, h].astype(F32)
            parts.append(value)
        return jnp.concatenate(parts, axis=1)

    rz = remote(ZS, ZR, rz_s, rz_r, zpartner)

    def rs_partner():
        ZS[...] = rs_total(1).astype(BF16)
        rz.start()

    final = remote(xs, xr, fs_s, fs_r, sibling)

    def rs_own():
        total = rs_total(0)
        rz.wait_recv()
        total = total + ZR[...].astype(F32)
        first, second = total[0:8, :], total[8:16, :]
        xs[...] = jnp.where(c == 0, second, first)
        final.start()
        final.wait()
        mine = jnp.where(c == 0, first, second)
        other = xr[...]
        rows_ref[0] = (combine * jnp.where(c == 0, mine, other)).astype(BF16)
        rows_ref[1] = jnp.where(c == 0, other, mine).astype(BF16)

    def weight_part(m):
        a = 0 if m < 2 else 1
        if m == 0:
            for ph in range(2):
                for r in range(1, NX):
                    t_copy(oc, r, ph, tf_s, tf_r).wait_recv()
        total = jnp.dot(
            HT[0, m * FP:(m + 1) * FP, :], G[a, :, xcols[0]],
            preferred_element_type=F32,
        )
        for r in range(1, NX):
            for ph in range(2):
                h_copy(ph, m, r).wait_recv()
            total = total + jnp.dot(
                HT[r, m * FP:(m + 1) * FP, :], TR[a, r - 1], preferred_element_type=F32
            )
        for d in range(NZ):
            DW[m, d] = total[:, d * 128:(d + 1) * 128]

    n = NZ - 1

    def z_copy(dr, m, d):
        return remote(
            SZ.at[dr, m, d], RZ.at[dr, m, d], z_s.at[dr, m, d], z_r.at[dr, m, d], znext[dr]
        )

    def z_sends(dr, d):
        return q < d if dr == 0 else q > d

    def z_gets(dr):
        return q > 0 if dr == 0 else q < NZ - 1

    left = {m: 0 for m in range(3)}
    stream = []
    for i in range(3 * n):
        ready = [m for m in range(3) if left[m] < n and (FIRST[m] <= i or m == 0)]
        ready = ready or [m for m in range(3) if left[m] < n]
        m = min(ready, key=lambda m: (left[m], m))
        stream.append((m, left[m]))
        left[m] += 1
    first_use = [min(i for i, v in enumerate(stream) if v[0] == m) for m in range(3)]

    def looked_up(i, which):
        value = jnp.int32(0)
        for k, v in enumerate(stream):
            if v[which]:
                value = jnp.where(i == k, v[which], value)
        return value

    def z_slot(slot, carry):
        for dr in range(2):
            i = slot - HOP * (q if dr == 0 else NZ - 1 - q)
            m, j = looked_up(i, 0), looked_up(i, 1)
            d = NZ - 1 - j if dr == 0 else j

            @pl.when((i >= 0) & (i < 3 * n) & z_sends(dr, d))
            def _():
                @pl.when(z_gets(dr))
                def _():
                    z_copy(dr, m, d).wait_recv()
                value = DW[m, d] + jnp.where(z_gets(dr), RZ[dr, m, d].astype(F32), 0.0)
                SZ[dr, m, d] = value.astype(BF16)
                z_copy(dr, m, d).start()
        return carry

    slots = 3 * n + HOP * n
    marks = {}
    rs_open(1)
    rs_open(0)
    later = [functools.partial(rs_step, ph, k) for k in range(2, NK + 1) for ph in (1, 0)]
    later += [rs_partner]
    for i, f in enumerate(later):
        marks.setdefault(min(1 + 2 * i, slots - 1), []).append(f)
    begin = 0
    for slot in range(slots + 1):
        here = marks.get(slot, [])
        dw = slot in first_use
        if (here or dw or slot == slots) and slot > begin:
            lax.fori_loop(begin, slot, z_slot, 0)
            begin = slot
        if dw:
            weight_part(first_use.index(slot))
        for f in here:
            f()
    rs_own()
    for m in range(3):
        value = DW[m, q]
        for dr in range(2):
            @pl.when(z_gets(dr))
            def _():
                z_copy(dr, m, q).wait_recv()
            value = value + jnp.where(z_gets(dr), RZ[dr, m, q].astype(F32), 0.0)
        wgrad_ref[m] = value[:F, :].astype(BF16)

    for cp in started:
        cp.wait_send()
    for ph in range(2):
        for m in range(3):
            for r in range(1, NX):
                h_copy(ph, m, r).wait_send()
    rz.wait_send()
    for ph in range(2):
        ref = G.at[c, rows_all(ph), :]
        remote(ref, ref, sib_s.at[ph], sib_r.at[ph], sibling).wait_send()
        for r in range(1, NX):
            t_copy(c, r, ph, t_s, t_r).wait_send()
    for dr in range(2):
        def drain(i, carry):
            m, d = i // NZ, i % NZ

            @pl.when(z_sends(dr, d))
            def _():
                z_copy(dr, m, d).wait_send()
            return carry
        lax.fori_loop(0, 3 * NZ, drain, 0)


def body(sizes, tokens, row_gate, block_mask, weights, out_grad):
    NX, NZ, NY = sizes
    NK = NY // 2
    D = tokens.shape[1]
    F = weights.shape[1]
    FP = -(-F // 16) * 16
    T = NY * 32
    gate = row_gate.reshape(1, 8)
    vmem = pl.BlockSpec(memory_space=pltpu.VMEM)
    hbm = pl.BlockSpec(memory_space=pltpu.HBM)
    dma = pltpu.SemaphoreType.DMA
    V = pltpu.VMEM
    rows, weight_grad = pl.pallas_call(
        functools.partial(kernel, sizes),
        out_shape=(
            jax.ShapeDtypeStruct((2, 8, D), BF16),
            jax.ShapeDtypeStruct((3, F, 128), BF16),
        ),
        in_specs=[hbm, hbm, vmem, pl.BlockSpec(memory_space=pltpu.SMEM), hbm],
        out_specs=(vmem, vmem),
        scratch_shapes=[
            V((8, D), F32), V((8, D), F32),
            V((2, T, D), BF16),
            V((2, NX - 1, T, D // NX), BF16),
            V((3, F, D), BF16),
            V((NX, 3 * FP, T), BF16),
            V((3, T, F), BF16),
            V((2, T, D), BF16), V((T, D), BF16),
            V((2, 2, NK, 2, 16, D // 2), BF16), V((2, 2, NK, 2, 16, D // 2), BF16),
            V((16, D), BF16), V((16, D), BF16),
            V((3, NZ, FP, 128), F32),
            V((2, 3, NZ, FP, 128), BF16), V((2, 3, NZ, FP, 128), BF16),
            V((2, 8, D), BF16), dma((2,)),
            dma, dma, dma, dma((2,)), dma((2,)),
            dma((2, 2, NK, 2)), dma((2, 2, NK, 2)),
            dma((2,)), dma((2,)),
            dma((NX - 1, 2)), dma((NX - 1, 2)),
            dma((NX - 1, 2)), dma((NX - 1, 2)),
            dma((2, 3, NX - 1)), dma((2, 3, NX - 1)),
            dma((2,)), dma((2,)),
            dma((2, 2, NK, 2)), dma((2, 2, NK, 2)),
            dma, dma, dma, dma,
            dma((2, 3, NZ)), dma((2, 3, NZ)),
        ],
        compiler_params=pltpu.CompilerParams(
            collective_id=0, has_side_effects=True, vmem_limit_bytes=60 << 20
        ),
        cost_estimate=pl.CostEstimate(flops=9 * 2 * T * D * F, bytes_accessed=8 * D * F, transcendentals=T * F),
    )(tokens, out_grad, gate, block_mask, weights)
    return rows[0], rows[1], weight_grad


def solution(mesh):
    in_specs = (
        P(("dp", "expert"), None),
        P(("dp", "expert")),
        P("dp"),
        P(None, "expert", None),
        P(("dp", "expert"), None),
    )
    out_specs = (P(("dp", "expert"), None), P(("dp", "expert"), None), P(None, "expert", "dp"))
    return jax.shard_map(
        functools.partial(body, SIZES), mesh=mesh, in_specs=in_specs, out_specs=out_specs, check_vma=False
    )
```

```python
import functools

import jax
import jax.numpy as jnp
from jax import lax
from jax.experimental import pallas as pl
from jax.experimental.pallas import tpu as pltpu
from jax.sharding import PartitionSpec as P

MESH = pl.DeviceIdType.MESH
F32 = jnp.float32
BF16 = jnp.bfloat16

SIZES = (4, 6, 8)
HOP = 3
FIRST = (0, 2, 4)
EARLY = True
STEPS = (1, 2, 3)


def kernel(
    sizes, tok_hbm, og_hbm, gate_ref, mask_ref, w_hbm, rows_ref, wgrad_ref,
    xs, xr, G, TR, W, HT, HR, TERM, SIB, SB, RB, ZS, ZR, DW, SZ, RZ,
    in_v, in_sem, w_sem, xs_s, xs_r, az_s, az_r, ag_s, ag_r, sib_s, sib_r, t_s, t_r, tf_s, tf_r,
    h_s, h_r, ts_s, ts_r, rs_s, rs_r, rz_s, rz_r, fs_s, fs_r, z_s, z_r,
):
    NX, NZ, NY = sizes
    NK = NY // 2
    D = tok_hbm.shape[1]
    F = W.shape[1]
    FP = HT.shape[1] // 3
    T = G.shape[1]
    HALF = D // 2
    XC = D // NX
    ZROWS = NY * 16

    dp = lax.axis_index("dp")
    ex = lax.axis_index("expert")
    x, q = dp // NZ, dp % NZ
    zh, y, c = ex // (2 * NY), (ex // 2) % NY, ex % 2
    oc, oz = 1 - c, 1 - zh
    zhp = (zh, oz)

    def at(x=x, q=q, zh=zh, y=y, c=c):
        return (x * NZ + q, zh * (2 * NY) + y * 2 + c)

    def remote(src, dst, ss, rs, to):
        return pltpu.make_async_remote_copy(
            src_ref=src, dst_ref=dst, send_sem=ss, recv_sem=rs, device_id=to, device_id_type=MESH
        )

    sibling = at(c=oc)
    zpartner = at(zh=oz)
    ynext = (at(y=(y + 1) % NY), at(y=(y + NY - 1) % NY))
    xnext = [at(x=(x + r) % NX) for r in range(1, NX)]
    znext = (at(q=(q + 1) % NZ), at(q=(q + NZ - 1) % NZ))

    w_copy = pltpu.make_async_copy(w_hbm, W, w_sem)
    loads = [pltpu.make_async_copy(r, in_v.at[i], in_sem.at[i]) for i, r in enumerate((tok_hbm, og_hbm))]
    for cp in loads:
        cp.start()
    w_copy.start()

    barrier = pltpu.get_barrier_semaphore()
    partners = [sibling, zpartner, *ynext, *xnext, *znext]
    for p in partners:
        pl.semaphore_signal(barrier, inc=1, device_id=p, device_id_type=MESH)

    for cp in loads:
        cp.wait()
    tok = in_v[0].astype(F32)
    spot = (lax.broadcasted_iota(jnp.int32, (8, 8), 0), lax.broadcasted_iota(jnp.int32, (8, 8), 1))
    gates = jnp.broadcast_to(gate_ref[...].astype(F32), (8, 8))
    combine = jnp.sum(jnp.where(spot[0] == spot[1], gates, 0.0), axis=1, keepdims=True)
    rg = (combine * in_v[1].astype(F32)).astype(BF16).astype(F32)
    xs[...] = jnp.where(c == 0, rg, tok)
    pl.semaphore_wait(barrier, len(partners))

    swap = remote(xs, xr, xs_s, xs_r, sibling)
    swap.start()
    swap.wait()
    got = xr[...]
    own = jnp.where(c == 0, tok, rg)
    block = jnp.concatenate([jnp.where(c == 0, own, got), jnp.where(c == 0, got, own)], axis=0)

    def place(o):
        return 0 if o == 0 else (2 * NK - 1 if abs(o) == NK else 2 * abs(o) - (o < 0))

    def rows_at(ph, first, n=1):
        return pl.ds(ph * ZROWS + first * 16, n * 16)

    def rows_of(ph, o):
        return rows_at(ph, place(o))

    def rows_all(ph):
        return pl.ds(ph * ZROWS, ZROWS)

    def half_of(h):
        return pl.ds(h * HALF, HALF)

    G[c, 0:16, :] = block.astype(BF16)

    def sgn(dr):
        return 1 if dr == 0 else -1

    def ag_copy(ph, dr, k, h):
        o = -sgn(dr)
        return remote(
            G.at[c, rows_of(ph, o * (k - 1)), half_of(h)], G.at[c, rows_of(ph, o * k), half_of(h)],
            ag_s.at[ph, dr, k - 1, h], ag_r.at[ph, dr, k - 1, h], ynext[dr],
        )

    started = []

    def ag_send(ph, dr, k, h):
        cp = ag_copy(ph, dr, k, h)
        cp.start()
        started.append(cp)

    def spread(ph, first, n):
        rows = rows_at(ph, first, n)
        ref = G.at[c, rows, :]
        remote(ref, ref, sib_s.at[ph], sib_r.at[ph], sibling).start()
        for r in range(1, NX):
            remote(
                G.at[c, rows, xcols[r]], TR.at[c, r - 1, rows, :],
                t_s.at[r - 1, ph], t_r.at[r - 1, ph], xnext[r - 1],
            ).start()

    xcols = [pl.ds(pl.multiple_of(((x + r) % NX) * XC, 128), XC) for r in range(NX)]

    def ag_has(dr, k, h):
        return k < NK or h == dr

    def az_copy(h):
        return remote(
            G.at[c, rows_of(0, 0), half_of(h)], G.at[c, rows_of(1, 0), half_of(h)], az_s.at[h], az_r.at[h], zpartner
        )

    def ag_first(ph):
        for h in range(2):
            if ph == 1:
                az_copy(h).wait_recv()
            for dr in range(2):
                if ag_has(dr, 1, h):
                    ag_send(ph, dr, 1, h)

    def ag_step(ph, k):
        for h in range(2):
            for dr in range(2):
                if not ag_has(dr, k, h):
                    continue
                ag_copy(ph, dr, k, h).wait_recv()
                if k < NK and ag_has(dr, k + 1, h):
                    ag_send(ph, dr, k + 1, h)
        if (ph, k) in BATCH:
            first, n = BATCH[ph, k]
            spread(ph, first, n)

    BATCH = {}
    for ph in range(2):
        begin = 0
        for k in STEPS:
            if k < NK:
                BATCH[ph, k] = (begin, 2 * k + 1 - begin)
                begin = 2 * k + 1
        BATCH[ph, NK] = (begin, 2 * NK - begin)

    for h in range(2):
        cp = az_copy(h)
        cp.start()
        started.append(cp)

    def contract(m, a, ph):
        rows = rows_all(ph)

        def step(i, acc):
            cols = pl.ds(pl.multiple_of(i * XC, 128), XC)
            return acc + lax.dot_general(
                W[m, :, cols], G[a, rows, cols], (((1,), (1,)), ((), ())), preferred_element_type=F32
            )
        return lax.fori_loop(0, NX, step, jnp.zeros((F, ZROWS), F32))

    def h_copy(ph, m, r):
        spot = (pl.ds(m * FP, FP), rows_all(ph))
        return remote(
            HT.at[0, *spot], HT.at[r, *spot], h_s.at[ph, m, r - 1], h_r.at[ph, m, r - 1], xnext[r - 1]
        )

    held = {}

    def hidden_first(ph):
        ref = G.at[oc, rows_all(ph), :]
        remote(ref, ref, sib_s.at[ph], sib_r.at[ph], sibling).wait_recv()
        if ph == 0:
            w_copy.wait()
        held[ph] = contract(0, 0, ph), contract(1, 0, ph)

    def hidden_second(ph):
        pre_gate, pre_up = held[ph]
        back = contract(2, 1, ph)
        live = mask_ref[zhp[ph]].astype(F32)
        sig = jax.nn.sigmoid(pre_gate)
        silu = pre_gate * sig
        hidden = live * silu * pre_up
        gate_grad = live * back * pre_up * (sig * (1.0 + pre_gate * (1.0 - sig)))
        up_grad = live * back * silu
        pad = jnp.zeros((FP - F, ZROWS), F32)
        lanes = rows_all(ph)
        for m, v in enumerate((gate_grad, up_grad, hidden)):
            HT[0, m * FP:(m + 1) * FP, lanes] = jnp.concatenate([v, pad], axis=0).astype(BF16)
            for r in range(1, NX):
                h_copy(ph, m, r).start()
        for m, v in enumerate((gate_grad, up_grad, hidden)):
            HR[m, rows_all(ph), :] = v.T.astype(BF16)

    ag_first(0)
    late0 = [(0, k) for k in range(NK // 2 + 1, NK + 1)]
    late1 = [(1, k) for k in range(1, NK + 1)]
    order = [(0, k) for k in range(1, NK // 2 + 1)] + [(1, 0)]
    while late0 or late1:
        if late0:
            order.append(late0.pop(0))
        if late1:
            order.append(late1.pop(0))
    work = [functools.partial(hidden_first, 0), functools.partial(hidden_second, 0)]
    for ph, k in order:
        if k == 0:
            ag_first(1)
        else:
            ag_step(ph, k)
        if EARLY and ph == 1 and k >= NK - 2 and work:
            work.pop(0)()
    work += [functools.partial(hidden_first, 1), functools.partial(hidden_second, 1)]
    for f in work:
        f()

    def terms(ph):
        rows = rows_all(ph)

        def step(i, carry):
            cols = pl.ds(pl.multiple_of(i * XC, 128), XC)
            dot = functools.partial(jnp.dot, preferred_element_type=F32)
            TERM[0, rows, cols] = dot(HR[2, rows, :], W[2, :, cols]).astype(BF16)
            TERM[1, rows, cols] = (
                dot(HR[0, rows, :], W[0, :, cols]) + dot(HR[1, rows, :], W[1, :, cols])
            ).astype(BF16)
            return carry

        lax.fori_loop(0, NX, step, 0)
        cp = remote(TERM.at[oc, rows, :], SIB.at[rows, :], ts_s.at[ph], ts_r.at[ph], sibling)
        cp.start()
        started.append(cp)
        return cp

    term_copies = {ph: terms(ph) for ph in (1, 0)}

    def t_copy(a, r, ph, ss, rs):
        ref = TR.at[a, r - 1, rows_all(ph), :]
        return remote(ref, ref, ss.at[r - 1, ph], rs.at[r - 1, ph], sibling)

    for ph in range(2):
        for r in range(1, NX):
            t_copy(c, r, ph, t_s, t_r).wait_recv()
            cp = t_copy(c, r, ph, tf_s, tf_r)
            cp.start()
            started.append(cp)

    def shares(ph, o, h):
        rows = rows_of(ph, o)
        return TERM[c, rows, half_of(h)].astype(F32) + SIB[rows, half_of(h)].astype(F32)

    def rs_has(dr, k, h):
        return k >= 1 and (k > 1 or h == dr)

    def rs_copy(ph, dr, k, h):
        return remote(
            SB.at[ph, dr, k - 1, h], RB.at[ph, dr, k - 1, h],
            rs_s.at[ph, dr, k - 1, h], rs_r.at[ph, dr, k - 1, h], ynext[dr],
        )

    def rs_send(ph, dr, k, h):
        value = shares(ph, sgn(dr) * (NK + 1 - k), h)
        if rs_has(dr, k - 1, h):
            rs_copy(ph, dr, k - 1, h).wait_recv()
            value = value + RB[ph, dr, k - 2, h].astype(F32)
        SB[ph, dr, k - 1, h] = value.astype(BF16)
        cp = rs_copy(ph, dr, k, h)
        cp.start()
        started.append(cp)

    def rs_open(ph):
        term_copies[ph].wait_recv()
        for dr in range(2):
            rs_send(ph, dr, 1, dr)
        for dr in range(2):
            rs_send(ph, dr, 2, 1 - dr)

    def rs_step(ph, k):
        for h in range(2):
            for dr in range(2):
                if k > 2 or h == dr:
                    rs_send(ph, dr, k, h)

    def rs_total(ph):
        parts = []
        for h in range(2):
            value = shares(ph, 0, h)
            for dr in range(2):
                if rs_has(dr, NK, h):
                    rs_copy(ph, dr, NK, h).wait_recv()
                    value = value + RB[ph, dr, NK - 1, h].astype(F32)
            parts.append(value)
        return jnp.concatenate(parts, axis=1)

    rz = remote(ZS, ZR, rz_s, rz_r, zpartner)

    def rs_partner():
        ZS[...] = rs_total(1).astype(BF16)
        rz.start()

    final = remote(xs, xr, fs_s, fs_r, sibling)

    def rs_own():
        total = rs_total(0)
        rz.wait_recv()
        total = total + ZR[...].astype(F32)
        first, second = total[0:8, :], total[8:16, :]
        xs[...] = jnp.where(c == 0, second, first)
        final.start()
        final.wait()
        mine = jnp.where(c == 0, first, second)
        other = xr[...]
        rows_ref[0] = (combine * jnp.where(c == 0, mine, other)).astype(BF16)
        rows_ref[1] = jnp.where(c == 0, other, mine).astype(BF16)

    def weight_part(m):
        a = 0 if m < 2 else 1
        if m == 0:
            for ph in range(2):
                for r in range(1, NX):
                    t_copy(oc, r, ph, tf_s, tf_r).wait_recv()
        total = jnp.dot(
            HT[0, m * FP:(m + 1) * FP, :], G[a, :, xcols[0]],
            preferred_element_type=F32,
        )
        for r in range(1, NX):
            for ph in range(2):
                h_copy(ph, m, r).wait_recv()
            total = total + jnp.dot(
                HT[r, m * FP:(m + 1) * FP, :], TR[a, r - 1], preferred_element_type=F32
            )
        for d in range(NZ):
            DW[m, d] = total[:, d * 128:(d + 1) * 128]

    n = NZ - 1

    def z_copy(dr, m, d):
        return remote(
            SZ.at[dr, m, d], RZ.at[dr, m, d], z_s.at[dr, m, d], z_r.at[dr, m, d], znext[dr]
        )

    def z_sends(dr, d):
        return q < d if dr == 0 else q > d

    def z_gets(dr):
        return q > 0 if dr == 0 else q < NZ - 1

    left = {m: 0 for m in range(3)}
    stream = []
    for i in range(3 * n):
        ready = [m for m in range(3) if left[m] < n and (FIRST[m] <= i or m == 0)]
        ready = ready or [m for m in range(3) if left[m] < n]
        m = min(ready, key=lambda m: (left[m], m))
        stream.append((m, left[m]))
        left[m] += 1
    first_use = [min(i for i, v in enumerate(stream) if v[0] == m) for m in range(3)]

    def looked_up(i, which):
        value = jnp.int32(0)
        for k, v in enumerate(stream):
            if v[which]:
                value = jnp.where(i == k, v[which], value)
        return value

    def z_slot(slot, carry):
        for dr in range(2):
            i = slot - HOP * (q if dr == 0 else NZ - 1 - q)
            m, j = looked_up(i, 0), looked_up(i, 1)
            d = NZ - 1 - j if dr == 0 else j

            @pl.when((i >= 0) & (i < 3 * n) & z_sends(dr, d))
            def _():
                @pl.when(z_gets(dr))
                def _():
                    z_copy(dr, m, d).wait_recv()
                value = DW[m, d] + jnp.where(z_gets(dr), RZ[dr, m, d].astype(F32), 0.0)
                SZ[dr, m, d] = value.astype(BF16)
                z_copy(dr, m, d).start()
        return carry

    slots = 3 * n + HOP * n
    marks = {}
    rs_open(1)
    rs_open(0)
    later = [functools.partial(rs_step, ph, k) for k in range(2, NK + 1) for ph in (1, 0)]
    later += [rs_partner]
    for i, f in enumerate(later):
        marks.setdefault(min(2 * i, slots - 1), []).append(f)
    begin = 0
    for slot in range(slots + 1):
        here = marks.get(slot, [])
        dw = slot in first_use
        if (here or dw or slot == slots) and slot > begin:
            lax.fori_loop(begin, slot, z_slot, 0)
            begin = slot
        if dw:
            weight_part(first_use.index(slot))
        for f in here:
            f()
    rs_own()
    for m in range(3):
        value = DW[m, q]
        for dr in range(2):
            @pl.when(z_gets(dr))
            def _():
                z_copy(dr, m, q).wait_recv()
            value = value + jnp.where(z_gets(dr), RZ[dr, m, q].astype(F32), 0.0)
        wgrad_ref[m] = value[:F, :].astype(BF16)

    for cp in started:
        cp.wait_send()
    for ph in range(2):
        for m in range(3):
            for r in range(1, NX):
                h_copy(ph, m, r).wait_send()
    rz.wait_send()
    for ph in range(2):
        ref = G.at[c, rows_all(ph), :]
        remote(ref, ref, sib_s.at[ph], sib_r.at[ph], sibling).wait_send()
        for r in range(1, NX):
            t_copy(c, r, ph, t_s, t_r).wait_send()
    for dr in range(2):
        def drain(i, carry):
            m, d = i // NZ, i % NZ

            @pl.when(z_sends(dr, d))
            def _():
                z_copy(dr, m, d).wait_send()
            return carry
        lax.fori_loop(0, 3 * NZ, drain, 0)


def body(sizes, tokens, row_gate, block_mask, weights, out_grad):
    NX, NZ, NY = sizes
    NK = NY // 2
    D = tokens.shape[1]
    F = weights.shape[1]
    FP = -(-F // 16) * 16
    T = NY * 32
    gate = row_gate.reshape(1, 8)
    vmem = pl.BlockSpec(memory_space=pltpu.VMEM)
    hbm = pl.BlockSpec(memory_space=pltpu.HBM)
    dma = pltpu.SemaphoreType.DMA
    V = pltpu.VMEM
    rows, weight_grad = pl.pallas_call(
        functools.partial(kernel, sizes),
        out_shape=(
            jax.ShapeDtypeStruct((2, 8, D), BF16),
            jax.ShapeDtypeStruct((3, F, 128), BF16),
        ),
        in_specs=[hbm, hbm, vmem, pl.BlockSpec(memory_space=pltpu.SMEM), hbm],
        out_specs=(vmem, vmem),
        scratch_shapes=[
            V((8, D), F32), V((8, D), F32),
            V((2, T, D), BF16),
            V((2, NX - 1, T, D // NX), BF16),
            V((3, F, D), BF16),
            V((NX, 3 * FP, T), BF16),
            V((3, T, F), BF16),
            V((2, T, D), BF16), V((T, D), BF16),
            V((2, 2, NK, 2, 16, D // 2), BF16), V((2, 2, NK, 2, 16, D // 2), BF16),
            V((16, D), BF16), V((16, D), BF16),
            V((3, NZ, FP, 128), F32),
            V((2, 3, NZ, FP, 128), BF16), V((2, 3, NZ, FP, 128), BF16),
            V((2, 8, D), BF16), dma((2,)),
            dma, dma, dma, dma((2,)), dma((2,)),
            dma((2, 2, NK, 2)), dma((2, 2, NK, 2)),
            dma((2,)), dma((2,)),
            dma((NX - 1, 2)), dma((NX - 1, 2)),
            dma((NX - 1, 2)), dma((NX - 1, 2)),
            dma((2, 3, NX - 1)), dma((2, 3, NX - 1)),
            dma((2,)), dma((2,)),
            dma((2, 2, NK, 2)), dma((2, 2, NK, 2)),
            dma, dma, dma, dma,
            dma((2, 3, NZ)), dma((2, 3, NZ)),
        ],
        compiler_params=pltpu.CompilerParams(
            collective_id=0, has_side_effects=True, vmem_limit_bytes=60 << 20
        ),
        cost_estimate=pl.CostEstimate(flops=9 * 2 * T * D * F, bytes_accessed=8 * D * F, transcendentals=T * F),
    )(tokens, out_grad, gate, block_mask, weights)
    return rows[0], rows[1], weight_grad


def solution(mesh):
    in_specs = (
        P(("dp", "expert"), None),
        P(("dp", "expert")),
        P("dp"),
        P(None, "expert", None),
        P(("dp", "expert"), None),
    )
    out_specs = (P(("dp", "expert"), None), P(("dp", "expert"), None), P(None, "expert", "dp"))
    return jax.shard_map(
        functools.partial(body, SIZES), mesh=mesh, in_specs=in_specs, out_specs=out_specs, check_vma=False
    )
```
